32 devices in a mesh: groups: 1, ep: 32 (over z, y, x, core).
Axes of the slice: x: 2, y: 2, z: 4, core: 2. Of those that a mesh axis runs over, the one named last changes fastest.
Arguments:
- hidden_in: bfloat16 [640, 2048], P(('groups', 'ep')), may hold values from -6 to 6
- queries: bfloat16 [640, 2048], P(('groups', 'ep')), may hold values from -6 to 6
- key_rows: bfloat16 [640, 2048], P(('groups', 'ep')), may hold values from -6 to 6
- value_rows: bfloat16 [640, 2048], P(('groups', 'ep')), may hold values from -6 to 6
- output_gate: bfloat16 [640, 2048], P(('groups', 'ep')), may hold values from -6 to 6
- decay_rate: float32 [640, 16], P(('groups', 'ep')), may hold values from 0.2 to 1
- write_rate: float32 [640, 16], P(('groups', 'ep')), may hold values from 0.1 to 1
- state_cache: bfloat16 [128, 16, 128, 128], P(('groups', 'ep')), may hold values from -6 to 6
- head_gain: float32 [128], replicated, may hold values from 0.25 to 1.75
- post_gain: float32 [2048], replicated, may hold values from 0.25 to 1.75
- routes: int32 [640, 10], P(('groups', 'ep')), may hold values from 0 to 31, all different within a row; in each aligned block of 20 rows (0 to 19, 20 to 39, ...) at most 7 rows name the same one
- route_weight: float32 [640, 10], P(('groups', 'ep')), may hold values from 0.05 to 0.3
- w_gate_up: bfloat16 [32, 2048, 1024], P('ep'), may hold values from -0.125 to 0.125
- w_down: bfloat16 [32, 512, 2048], P('ep'), may hold values from -0.25 to 0.25
Outputs:
- layer_out: bfloat16 [640, 2048], P(('groups', 'ep'))
The draws below stay inside these ranges and needn't reach their ends.
Inputs may be any that keep to these rules, and one draw needn't show every extreme that they name: `routes`: in each aligned block of 20 rows (the rows of one device) a row names 10 different experts and no expert is named more than 7 times; in every draw some expert is named exactly 7 times in some block.
All inputs are finite; a program needn't handle non-finite values.
Results may differ from the reference program's by a relative error of at most 0.0037.
Values may be sent and summed in bfloat16 or wider, within the bound.
A program may use at most 64 MiB of HBM per device.

```python
import math
import jax
import jax.numpy as jnp
import numpy as np
from jax import lax

HEADS = 16
HEAD_DIM = 128
D = 2048
FF = 512
TOP = 10
SEQ_DEV = 4
ROWS_DEV = 20
EXPERTS = 32
CAP = 7
SEQS = 128
TOKENS = 640
N_EP = 32


def steps_of(own_key, extent, cuts, smallest, largest):
    def one(axis_at, parts):
        steps = jax.random.uniform(jax.random.fold_in(jax.random.fold_in(own_key, 6), axis_at), (parts,), jnp.float32, smallest / len(cuts), largest / len(cuts))
        return jnp.repeat(jnp.exp(steps), extent[axis_at] // parts).reshape((-1,) + (1,) * (len(extent) - axis_at - 1))

    factor_of = one(*cuts[0])
    for cut in cuts[1:]:
        factor_of = factor_of * one(*cut)
    return factor_of


def routed_block(rng, own, number, rows, count, top, reach, lean):
    ranking = jax.random.permutation(rng, count)
    crowded, usual = shares(count, rows * top, reach, lean, True), shares(count, rows * top, reach, lean, False)
    places = jnp.arange(count)

    def named(tallies, offset_by):
        used = int((tallies > 0).sum())
        fixed = max(1, used // 4)
        passed = fixed + (places - fixed + offset_by * (used - fixed)) % max(1, count - fixed)
        return jnp.zeros((count,), jnp.int32).at[ranking[jnp.where(places < fixed, places, passed)]].set(jnp.asarray(tallies, jnp.int32))

    tallies = jnp.where(number % 4 == 0, named(crowded, number // 4), named(usual, number - number // 4 - 1))
    mixed = jax.random.permutation(jax.random.fold_in(own, 3), count)
    source_of, taker = mixed[0:count // 2 * 2:2], mixed[1:count // 2 * 2:2]
    room = jnp.minimum(tallies[source_of] - 1, reach - tallies[taker]) // 2
    room = jnp.where((source_of == ranking[0]) | (taker == ranking[0]) | (tallies[taker] == 0), 0, jnp.maximum(room, 0))
    passed = jax.random.randint(jax.random.fold_in(own, 4), (count // 2,), 0, 1 << 20) % (room + 1)
    tallies = tallies.at[source_of].add(-passed).at[taker].add(passed)
    items = jnp.searchsorted(jnp.cumsum(tallies), jnp.arange(rows * top), side="right").astype(jnp.int32)
    table = items.reshape(top, rows).T
    table = table[jax.random.permutation(jax.random.fold_in(own, 1), rows)]
    offset_by = jax.random.randint(jax.random.fold_in(own, 2), (rows, 1), 0, top)
    return jnp.take_along_axis(table, (jnp.arange(top)[None, :] + offset_by) % top, axis=1)


def shares(amount, total, bound, lean, full):
    loads = [(1 << 20) // math.isqrt(grade ** lean) + 1 for grade in range(1, amount + 1)]
    largest = bound if full else min(bound, max(-(-total // amount), total * loads[0] // sum(loads)))
    least = 1 if total - largest >= amount - 1 else 0
    counts, surplus = [largest] + [least] * (amount - 1), total - largest - least * (amount - 1)
    while surplus > 0:
        movable = [i for i in range(1, amount) if counts[i] < largest] or [i for i in range(1, amount) if counts[i] < bound]
        pool, budget = sum([loads[i] for i in movable]), surplus
        for i in movable:
            addition = min(bound - counts[i], max(1, budget * loads[i] // pool), surplus)
            counts[i] = counts[i] + addition
            surplus = surplus - addition
    return np.array(counts)


def gaussian(key, extent, scale, bound, cuts=(), held_as=jnp.bfloat16):
    result = scale * jax.random.normal(key, extent, jnp.float32)
    if cuts:
        result = result * steps_of(key, extent, cuts, -0.22, 0.18)
    return jnp.clip(result, -bound, bound).astype(held_as)


def setup_inputs(seed: int = 0, part: int = 0) -> dict:
    arg_keys = jax.random.split(jax.random.key(seed), 15)
    part_splits = jax.random.split(jax.random.fold_in(arg_keys[14], part), 15)
    hidden_in = gaussian(part_splits[0], (TOKENS, D), 1.0, 6.0, ((0, 32),))
    queries = gaussian(part_splits[1], (TOKENS, D), 1.0, 6.0, ((0, 32),))
    key_rows = gaussian(part_splits[2], (TOKENS, D), 1.0, 6.0, ((0, 32),))
    value_rows = gaussian(part_splits[3], (TOKENS, D), 1.0, 6.0, ((0, 32),))
    output_gate = gaussian(part_splits[4], (TOKENS, D), 1.0, 6.0, ((0, 32),))
    decay_rate = jnp.clip(0.2 + 0.8 * jax.random.uniform(part_splits[5], (TOKENS, HEADS), jnp.float32) ** steps_of(part_splits[5], (TOKENS, HEADS), ((0, 32),), -0.2, 0.2), 0.2, 1.0)
    write_rate = jnp.clip(0.1 + 0.9 * jax.random.uniform(part_splits[6], (TOKENS, HEADS), jnp.float32) ** steps_of(part_splits[6], (TOKENS, HEADS), ((0, 32),), -0.2, 0.2), 0.1, 1.0)
    state_cache = gaussian(part_splits[7], (SEQS, HEADS, HEAD_DIM, HEAD_DIM), 1.0, 6.0, ((0, 32),))
    head_gain = jnp.clip(1.0 + 0.15 * jax.random.normal(arg_keys[8], (HEAD_DIM,), jnp.float32), 0.25, 1.75)
    post_gain = jnp.clip(1.0 + 0.15 * jax.random.normal(arg_keys[9], (D,), jnp.float32), 0.25, 1.75)
    routes_keys = jax.random.split(jax.random.fold_in(part_splits[10], 1), TOKENS // ROWS_DEV)
    routes_turns = jax.random.permutation(jax.random.fold_in(part_splits[10], 3), TOKENS // ROWS_DEV)
    routes = jax.vmap(lambda own, number: routed_block(jax.random.fold_in(part_splits[10], 2), own, number, ROWS_DEV, EXPERTS, TOP, CAP, 2))(routes_keys, routes_turns).reshape((TOKENS, TOP))
    route_weight = jnp.clip(0.05 + 0.25 * jax.random.uniform(part_splits[11], (TOKENS, TOP), jnp.float32) ** steps_of(part_splits[11], (TOKENS, TOP), ((0, 32),), -0.2, 0.2), 0.05, 0.3)
    w_gate_up = gaussian(arg_keys[12], (EXPERTS, D, 2 * FF), D ** -0.5, 0.125, ((0, 32),))
    w_down = gaussian(arg_keys[13], (EXPERTS, FF, D), FF ** -0.5, 0.25, ((0, 32),))
    return {"hidden_in": hidden_in, "queries": queries, "key_rows": key_rows, "value_rows": value_rows, "output_gate": output_gate, "decay_rate": decay_rate, "write_rate": write_rate, "state_cache": state_cache, "head_gain": head_gain, "post_gain": post_gain, "routes": routes, "route_weight": route_weight, "w_gate_up": w_gate_up, "w_down": w_down}


def normalize(vectors):
    return vectors / jnp.sqrt(lax.optimization_barrier(jnp.sum(vectors * vectors, -1, keepdims=True)) + 1e-06)

def attend(hidden_in, queries, key_rows, value_rows, output_gate, decay_rate, write_rate, state_cache, head_gain, post_gain):
    count, heads = decay_rate.shape
    seq_count = state_cache.shape[0]
    steps = count // seq_count
    head_dim = head_gain.shape[0]
    q_unit = normalize(queries.astype(jnp.float32).reshape(seq_count, steps, heads, head_dim))
    k_unit = normalize(key_rows.astype(jnp.float32).reshape(seq_count, steps, heads, head_dim))
    values = value_rows.astype(jnp.float32).reshape(seq_count, steps, heads, head_dim)
    gating = output_gate.astype(jnp.float32).reshape(count, heads, head_dim)
    decays = decay_rate.reshape(seq_count, steps, heads)
    writes = write_rate.reshape(seq_count, steps, heads)
    state = state_cache.astype(jnp.float32)
    outputs = []
    for step in range(steps):
        q_now = q_unit[:, step]
        k_now = k_unit[:, step]
        v_now = values[:, step]
        alpha = decays[:, step][..., None]
        beta = writes[:, step][..., None]
        stacked = jnp.stack([q_now, k_now], 1)
        reads = jnp.einsum('rshk,rhkv->rshv', stacked, state, precision=lax.Precision.HIGHEST, preferred_element_type=jnp.float32)
        q_read = reads[:, 0]
        k_read = reads[:, 1]
        intersection = lax.optimization_barrier(jnp.sum(q_now * k_now, -1, keepdims=True))
        outputs.append(alpha * q_read + beta * intersection * (v_now - alpha * k_read))
        state = alpha[..., None] * (state - beta[..., None] * k_now[..., None] * k_read[:, :, None, :]) + beta[..., None] * k_now[..., None] * v_now[:, :, None, :]
    attn = jnp.stack(outputs, 1).reshape(count, heads, head_dim)
    scale = lax.rsqrt(lax.optimization_barrier(jnp.mean(attn * attn, -1, keepdims=True)) + 1e-06)
    gated = attn * scale * head_gain * jax.nn.silu(gating)
    mixed = hidden_in.astype(jnp.float32) + gated.reshape(count, heads * head_dim)
    factor = lax.rsqrt(lax.optimization_barrier(jnp.mean(mixed * mixed, -1, keepdims=True)) + 1e-06)
    normed = (mixed * factor * post_gain).astype(jnp.bfloat16)
    return (mixed, normed)

def expert_apply(rows_in, gate_up, down):
    width = down.shape[0]
    product = jnp.dot(rows_in, gate_up, preferred_element_type=jnp.float32)
    hidden_units = (jax.nn.silu(product[:, :width]) * product[:, width:]).astype(jnp.bfloat16)
    return jnp.dot(hidden_units, down, preferred_element_type=jnp.float32).astype(jnp.bfloat16)

def reference(hidden_in, queries, key_rows, value_rows, output_gate, decay_rate, write_rate, state_cache, head_gain, post_gain, routes, route_weight, w_gate_up, w_down):

    def block_attend(pieces):
        return attend(*pieces, head_gain, post_gain)
    blocked = tuple((a.reshape((N_EP, ROWS_DEV) + a.shape[1:]) for a in (hidden_in, queries, key_rows, value_rows, output_gate, decay_rate, write_rate)))
    blocked = blocked + (state_cache.reshape((N_EP, SEQ_DEV) + state_cache.shape[1:]),)
    mixed, normed = lax.map(block_attend, blocked)
    mixed = mixed.reshape(TOKENS, D)
    normed = normed.reshape(TOKENS, D)
    flat_routes = routes.reshape(N_EP, ROWS_DEV * TOP)
    position = jnp.arange(ROWS_DEV * TOP, dtype=jnp.int32)
    earlier = (flat_routes[:, :, None] == flat_routes[:, None, :]) & (position[:, None] > position[None, :])[None]
    rank = lax.optimization_barrier(jnp.sum(earlier.astype(jnp.int32), -1)).astype(jnp.int32)
    block_id = jnp.broadcast_to(jnp.arange(N_EP, dtype=jnp.int32)[:, None], flat_routes.shape)
    row_id = (position // TOP)[None, :] + ROWS_DEV * block_id
    table = jnp.zeros((EXPERTS, N_EP, CAP), jnp.int32).at[flat_routes, block_id, rank].set(row_id)

    def run_expert(pieces):
        indices, gate_up, down = pieces
        return expert_apply(normed[indices.reshape(-1)], gate_up, down)
    results = lax.map(run_expert, (table, w_gate_up, w_down))
    weights = route_weight.reshape(N_EP, ROWS_DEV, TOP)

    def block_sum(pieces):
        experts_of, ranks_of, block_index, weight_block = pieces
        picked = results[experts_of, block_index * CAP + ranks_of].reshape(ROWS_DEV, TOP, D)
        return lax.optimization_barrier(jnp.sum(weight_block[..., None] * picked.astype(jnp.float32), 1))
    moe_sum = lax.map(block_sum, (flat_routes, rank, jnp.arange(N_EP, dtype=jnp.int32), weights))
    return (mixed + moe_sum.reshape(TOKENS, D)).astype(jnp.bfloat16)
```

```python
import functools

import jax
import jax.numpy as jnp
from jax import lax
from jax.experimental import pallas as pl
from jax.experimental.pallas import tpu as pltpu
from jax.sharding import PartitionSpec as P

F32 = jnp.float32
BF16 = jnp.bfloat16
LANE = 8
MESH = pl.DeviceIdType.MESH


def iota(shape, dim):
    return lax.broadcasted_iota(jnp.int32, shape, dim)


def exact_dot(a, b, dims=None):
    dims = dims or (((1,), (0,)), ((), ()))
    return lax.dot_general(a, b, dims, precision=lax.Precision.HIGHEST, preferred_element_type=F32)


def dot(a, b):
    return jnp.dot(a, b, preferred_element_type=F32)


def split(value):
    high = value.astype(BF16)
    return high, (value - high.astype(F32)).astype(BF16)


def kernel(
    n,
    steps,
    heads,
    head_dim,
    hidden_ref,
    q_ref,
    k_ref,
    v_ref,
    gate_ref,
    decay_ref,
    write_ref,
    state_ref,
    head_gain_ref,
    post_gain_ref,
    routes_ref,
    weight_ref,
    gate_up_hbm,
    down_hbm,
    out_ref,
    hid_s,
    q_s,
    k_s,
    v_s,
    gate_s,
    a_s,
    b_s,
    mixed_s,
    gate_up_s,
    down_s,
    out_buf,
    in_buf,
    back_buf,
    ret_buf,
    hidden_s,
    weight_sem,
    local_sem,
    send_sem,
    recv_sem,
):
    me = lax.axis_index("ep")
    rows, width = hidden_ref.shape
    top = routes_ref.shape[1]
    seqs = rows // steps
    packed = steps * LANE
    half = width // 2
    ff = down_s.shape[0]
    barrier = pltpu.get_barrier_semaphore()

    def greet(i, carry):
        pl.semaphore_signal(
            barrier, inc=1, device_id={"ep": lax.rem(me + i, n)}, device_id_type=MESH
        )
        return carry

    lax.fori_loop(1, n, greet, 0)
    gate_up_copy = pltpu.make_async_copy(gate_up_hbm.at[0], gate_up_s, weight_sem.at[0])
    down_copy = pltpu.make_async_copy(down_hbm.at[0], down_s, weight_sem.at[1])
    gate_up_copy.start()
    down_copy.start()

    new_row, old_row = iota((packed, rows), 0), iota((packed, rows), 1)
    place = (old_row // steps == new_row % LANE) & (old_row % steps == new_row // LANE)
    place_f = place.astype(F32)
    place_b = place_f.astype(BF16)
    hid_s[...] = dot(place_b, hidden_ref[...])
    q_s[...] = dot(place_b, q_ref[...])
    k_s[...] = dot(place_b, k_ref[...])
    v_s[...] = dot(place_b, v_ref[...])
    gate_s[...] = dot(place_b, gate_ref[...])
    spread = (iota((heads, width), 1) // head_dim == iota((heads, width), 0)).astype(F32)
    a_s[...] = exact_dot(exact_dot(place_f, decay_ref[...]), spread)
    b_s[...] = exact_dot(exact_dot(place_f, write_ref[...]), spread)
    gain = head_gain_ref[...]
    sequence = iota((2 * packed, head_dim), 0) % LANE

    def lanes_sum(value):
        return jnp.sum(value, -1, keepdims=True)

    def one_head(h):
        cols = pl.ds(pl.multiple_of(h * head_dim, head_dim), head_dim)
        k_all, q_all = k_s[:, cols], q_s[:, cols]
        both = jnp.concatenate([k_all, q_all], 0).astype(BF16)
        reads = jnp.zeros((2 * packed, head_dim), F32)
        for s in range(seqs):
            reads = jnp.where(sequence == s, dot(both, state_ref[s, h]), reads)
        carried = None
        writes, keys = [], []
        for t in range(steps):
            at = slice(t * LANE, (t + 1) * LANE)
            k, q = k_all[at], q_all[at]
            here = pl.ds(t * LANE, LANE)
            a, b, v = a_s[here, cols], b_s[here, cols], v_s[here, cols]
            k_scale = lax.rsqrt(lanes_sum(k * k) + 1e-06)
            q_scale = lax.rsqrt(lanes_sum(q * q) + 1e-06)
            k_read = reads[at] if t == 0 else carried * reads[at]
            for key, w in zip(keys, writes):
                k_read = k_read + lanes_sum(k * key) * w
            new = b * (v - a * (k_scale * k_read))
            carried = a if t == 0 else carried * a
            writes = [w * a for w in writes] + [new * k_scale]
            keys = keys + [k]
            attn = carried * reads[packed + t * LANE : packed + (t + 1) * LANE]
            for key, w in zip(keys, writes):
                attn = attn + lanes_sum(q * key) * w
            attn = attn * q_scale
            norm = lax.rsqrt(lanes_sum(attn * attn) * (1.0 / head_dim) + 1e-06)
            g = gate_s[here, cols]
            mixed_s[here, cols] = hid_s[here, cols] + attn * norm * gain * (g / (1.0 + jnp.exp(-g)))

    def head_group(i, carry):
        for j in range(2):
            one_head(2 * i + j)
        return carry

    lax.fori_loop(0, heads // 2, head_group, 0)
    mixed = mixed_s[...]
    factor = lax.rsqrt(jnp.sum(mixed * mixed, -1, keepdims=True) * (1.0 / width) + 1e-06)
    normed = (mixed * factor * post_gain_ref[...]).astype(BF16)

    expert = iota((rows, n), 1)
    named = jnp.zeros((rows, n), F32)
    weights = jnp.zeros((rows, n), F32)
    for j in range(top):
        hit = routes_ref[:, j : j + 1] == expert
        named = jnp.where(hit, 1.0, named)
        weights = jnp.where(hit, weight_ref[:, j : j + 1], weights)
    earlier = (iota((rows, rows), 0) >= iota((rows, rows), 1)).astype(BF16)
    order = named * dot(earlier, named.astype(BF16))
    order = dot(place_b, order.astype(BF16)).astype(BF16)
    weights = exact_dot(place_f, weights)

    slots = n * 16
    slot_row = iota((slots, n), 0)
    owner = (slot_row // 16 == iota((slots, n), 1)).astype(BF16)
    found = lax.dot_general(owner, order, (((1,), (1,)), ((), ())), preferred_element_type=F32)
    slot_at = iota((slots, packed), 0)
    chosen = found == (slot_at % 8 + 1).astype(F32)
    on_left = slot_at % 16 < 8
    pick_left = jnp.where(chosen & on_left, 1.0, 0.0).astype(BF16)
    pick_right = jnp.where(chosen & ~on_left, 1.0, 0.0).astype(BF16)
    step = 256
    for c in range(half // step):
        left = normed[:, c * step : (c + 1) * step]
        right = normed[:, half + c * step : half + (c + 1) * step]
        out_buf[:, c * step : (c + 1) * step] = (dot(pick_left, left) + dot(pick_right, right)).astype(BF16)

    def block(i):
        return pl.ds(pl.multiple_of(i * 16, 16), 16)

    def exchange(source, target, number):
        def send(i, carry):
            other = lax.rem(me + i, n)
            pltpu.make_async_remote_copy(
                src_ref=source.at[block(other)],
                dst_ref=target.at[block(me)],
                send_sem=send_sem.at[number],
                recv_sem=recv_sem.at[number],
                device_id={"ep": other},
                device_id_type=MESH,
            ).start()
            return carry

        lax.fori_loop(1, n, send, 0)
        own = pltpu.make_async_copy(source.at[block(me)], target.at[block(me)], local_sem.at[number])
        own.start()
        own.wait()
        rest = pl.ds(0, (n - 1) * 16)
        return pltpu.make_async_remote_copy(
            src_ref=source.at[rest],
            dst_ref=target.at[rest],
            send_sem=send_sem.at[number],
            recv_sem=recv_sem.at[number],
            device_id={"ep": lax.rem(me + 1, n)},
            device_id_type=MESH,
        )

    pl.semaphore_wait(barrier, n - 1)
    first = exchange(out_buf, in_buf, 0)
    owner_t = (iota((n, slots), 1) // 16 == iota((n, slots), 0)).astype(BF16)
    lane_slot = iota((packed, slots), 1)
    taken = dot(order, owner_t) == (lane_slot % 8 + 1).astype(F32)
    high, low = split(weights)
    lane_left = lane_slot % 16 < 8
    mixing = []
    for part in (high, low):
        value = dot(part, owner_t)
        mixing.append(jnp.where(taken & lane_left, value, 0.0).astype(BF16))
        mixing.append(jnp.where(taken & ~lane_left, value, 0.0).astype(BF16))
    mix = jnp.concatenate(mixing, 0)
    gate_up_copy.wait()
    down_copy.wait()
    first.wait_recv()

    arrived = in_buf[...].astype(F32).reshape(n, 16, half)
    left_in = arrived[:, :8].reshape(n * 8, half).astype(BF16)
    right_in = arrived[:, 8:].reshape(n * 8, half).astype(BF16)
    for c in range(ff // step):
        at = slice(c * step, (c + 1) * step)
        up_at = slice(ff + c * step, ff + (c + 1) * step)
        gate = dot(left_in, gate_up_s[:half, at]) + dot(right_in, gate_up_s[half:, at])
        up = dot(left_in, gate_up_s[:half, up_at]) + dot(right_in, gate_up_s[half:, up_at])
        hidden_s[:, at] = (gate / (1.0 + jnp.exp(-gate)) * up).astype(BF16)
    units = hidden_s[...]
    for c in range(half // step):
        at = slice(c * step, (c + 1) * step)
        right_at = slice(half + c * step, half + (c + 1) * step)
        left = dot(units, down_s[:, at]).reshape(n, 8, step)
        right = dot(units, down_s[:, right_at]).reshape(n, 8, step)
        back_buf[:, at] = jnp.concatenate([left, right], 1).reshape(slots, step).astype(BF16)
    second = exchange(back_buf, ret_buf, 1)
    first.wait_send()
    second.wait_recv()
    for c in range(half // step):
        at = slice(c * step, (c + 1) * step)
        right_at = slice(half + c * step, half + (c + 1) * step)
        sums = dot(mix, ret_buf[:, at])
        left = sums[:packed] + sums[2 * packed : 3 * packed]
        right = sums[packed : 2 * packed] + sums[3 * packed :]
        for cols, value in ((at, left), (right_at, right)):
            total = (mixed_s[:, cols] + value).astype(BF16)
            out_ref[:, cols] = lax.dot_general(
                place_b, total, (((0,), (0,)), ((), ())), preferred_element_type=F32
            ).astype(BF16)
    second.wait_send()


def per_device(
    hidden_in,
    queries,
    key_rows,
    value_rows,
    output_gate,
    decay_rate,
    write_rate,
    state_cache,
    head_gain,
    post_gain,
    routes,
    route_weight,
    w_gate_up,
    w_down,
):
    rows, width = hidden_in.shape
    n = lax.axis_size("ep")
    seqs, heads, head_dim, _ = state_cache.shape
    steps = rows // seqs
    packed = steps * LANE
    ff = w_down.shape[1]
    capacity = max(2, (rows * routes.shape[1] + n - 1) // n)
    assert capacity <= 8 and seqs <= LANE
    vmem = pl.BlockSpec(memory_space=pltpu.VMEM)
    anywhere = pl.BlockSpec(memory_space=pl.ANY)
    wide = pltpu.VMEM((packed, width), F32)
    blocks = pltpu.VMEM((n * 16, width // 2), BF16)
    return pl.pallas_call(
        functools.partial(kernel, n, steps, heads, head_dim),
        out_shape=jax.ShapeDtypeStruct((rows, width), BF16),
        in_specs=[vmem] * 12 + [anywhere] * 2,
        out_specs=vmem,
        scratch_shapes=[wide] * 8
        + [pltpu.VMEM(w_gate_up.shape[1:], BF16), pltpu.VMEM(w_down.shape[1:], BF16)]
        + [blocks] * 4
        + [
            pltpu.VMEM((n * 8, ff), BF16),
            pltpu.SemaphoreType.DMA((2,)),
            pltpu.SemaphoreType.DMA((2,)),
            pltpu.SemaphoreType.DMA((2,)),
            pltpu.SemaphoreType.DMA((2,)),
        ],
        compiler_params=pltpu.CompilerParams(
            collective_id=0, has_side_effects=True, vmem_limit_bytes=56 << 20
        ),
    )(
        hidden_in,
        queries,
        key_rows,
        value_rows,
        output_gate,
        decay_rate,
        write_rate,
        state_cache,
        head_gain.reshape(1, -1),
        post_gain.reshape(1, -1),
        routes,
        route_weight,
        w_gate_up,
        w_down,
    )


def solution(mesh):
    split_rows = P(("groups", "ep"), None)
    in_specs = (
        (split_rows,) * 7
        + (P(("groups", "ep"), None, None, None), P(), P(), split_rows, split_rows)
        + (P("ep", None, None), P("ep", None, None))
    )
    return jax.shard_map(
        per_device, mesh=mesh, in_specs=in_specs, out_specs=split_rows, check_vma=False
    )
```

```python
import functools

import jax
import jax.numpy as jnp
from jax import lax
from jax.experimental import pallas as pl
from jax.experimental.pallas import tpu as pltpu
from jax.sharding import PartitionSpec as P

F32 = jnp.float32
BF16 = jnp.bfloat16
LANE = 8
MESH = pl.DeviceIdType.MESH


def iota(shape, dim):
    return lax.broadcasted_iota(jnp.int32, shape, dim)


def exact_dot(a, b, dims=None):
    dims = dims or (((1,), (0,)), ((), ()))
    return lax.dot_general(a, b, dims, precision=lax.Precision.HIGHEST, preferred_element_type=F32)


def dot(a, b):
    return jnp.dot(a, b, preferred_element_type=F32)


def split(value):
    high = value.astype(BF16)
    return high, (value - high.astype(F32)).astype(BF16)


def kernel(
    n,
    steps,
    heads,
    head_dim,
    hidden_ref,
    q_ref,
    k_ref,
    v_ref,
    gate_ref,
    decay_ref,
    write_ref,
    state_ref,
    head_gain_ref,
    post_gain_ref,
    routes_ref,
    weight_ref,
    gate_up_hbm,
    down_hbm,
    out_ref,
    hid_s,
    q_s,
    k_s,
    v_s,
    gate_s,
    a_s,
    b_s,
    mixed_s,
    gate_up_s,
    down_s,
    out_buf,
    in_buf,
    back_buf,
    ret_buf,
    hidden_s,
    weight_sem,
    local_sem,
    send_sem,
    recv_sem,
):
    me = lax.axis_index("ep")
    rows, width = hidden_ref.shape
    top = routes_ref.shape[0]
    seqs = rows // steps
    packed = steps * LANE
    half = width // 2
    ff = down_s.shape[0]
    barrier = pltpu.get_barrier_semaphore()

    def greet(i, carry):
        pl.semaphore_signal(
            barrier, inc=1, device_id={"ep": lax.rem(me + i, n)}, device_id_type=MESH
        )
        return carry

    lax.fori_loop(1, n, greet, 0)
    gate_up_copy = pltpu.make_async_copy(gate_up_hbm.at[0], gate_up_s, weight_sem.at[0])
    down_copy = pltpu.make_async_copy(down_hbm.at[0], down_s, weight_sem.at[1])
    gate_up_copy.start()
    down_copy.start()

    new_row, old_row = iota((packed, rows), 0), iota((packed, rows), 1)
    place = (old_row // steps == new_row % LANE) & (old_row % steps == new_row // LANE)
    place_f = place.astype(F32)
    place_b = place_f.astype(BF16)
    hid_s[...] = dot(place_b, hidden_ref[...])
    q_s[...] = dot(place_b, q_ref[...])
    k_s[...] = dot(place_b, k_ref[...])
    v_s[...] = dot(place_b, v_ref[...])
    gate_s[...] = dot(place_b, gate_ref[...])
    spread = (iota((heads, width), 1) // head_dim == iota((heads, width), 0)).astype(F32)
    last = (((1,), (1,)), ((), ()))
    a_s[...] = exact_dot(exact_dot(place_f, decay_ref[...], last), spread)
    b_s[...] = exact_dot(exact_dot(place_f, write_ref[...], last), spread)
    gain = head_gain_ref[...]
    sequence = iota((2 * packed, head_dim), 0) % LANE

    def lanes_sum(value):
        return jnp.sum(value, -1, keepdims=True)

    def one_head(h):
        cols = pl.ds(pl.multiple_of(h * head_dim, head_dim), head_dim)
        k_all, q_all = k_s[:, cols], q_s[:, cols]
        both = jnp.concatenate([k_all, q_all], 0).astype(BF16)
        reads = jnp.zeros((2 * packed, head_dim), F32)
        for s in range(seqs):
            reads = jnp.where(sequence == s, dot(both, state_ref[s, h]), reads)
        carried = None
        writes, keys = [], []
        for t in range(steps):
            at = slice(t * LANE, (t + 1) * LANE)
            k, q = k_all[at], q_all[at]
            here = pl.ds(t * LANE, LANE)
            a, b, v = a_s[here, cols], b_s[here, cols], v_s[here, cols]
            k_scale = lax.rsqrt(lanes_sum(k * k) + 1e-06)
            q_scale = lax.rsqrt(lanes_sum(q * q) + 1e-06)
            k_read = reads[at] if t == 0 else carried * reads[at]
            for key, w in zip(keys, writes):
                k_read = k_read + lanes_sum(k * key) * w
            new = b * (v - a * (k_scale * k_read))
            carried = a if t == 0 else carried * a
            writes = [w * a for w in writes] + [new * k_scale]
            keys = keys + [k]
            attn = carried * reads[packed + t * LANE : packed + (t + 1) * LANE]
            for key, w in zip(keys, writes):
                attn = attn + lanes_sum(q * key) * w
            attn = attn * q_scale
            norm = lax.rsqrt(lanes_sum(attn * attn) * (1.0 / head_dim) + 1e-06)
            g = gate_s[here, cols]
            mixed_s[here, cols] = hid_s[here, cols] + attn * norm * gain * (g / (1.0 + jnp.exp(-g)))

    def head_group(i, carry):
        for j in range(4):
            one_head(4 * i + j)
        return carry

    lax.fori_loop(0, heads // 4, head_group, 0)
    mixed = mixed_s[...]
    factor = lax.rsqrt(jnp.sum(mixed * mixed, -1, keepdims=True) * (1.0 / width) + 1e-06)
    normed = (mixed * factor * post_gain_ref[...]).astype(BF16)

    expert = iota((n, rows), 0)
    named = jnp.zeros((n, rows), F32)
    weights = jnp.zeros((n, rows), F32)
    for j in range(top):
        hit = routes_ref[j : j + 1, :] == expert
        named = jnp.where(hit, 1.0, named)
        weights = jnp.where(hit, weight_ref[j : j + 1, :], weights)
    earlier = (iota((rows, rows), 0) <= iota((rows, rows), 1)).astype(BF16)
    order = named * dot(named.astype(BF16), earlier)
    order = lax.dot_general(order.astype(BF16), place_b, last, preferred_element_type=F32).astype(BF16)
    weights = exact_dot(weights, place_f, last)

    slots = n * 16
    slot_row = iota((slots, n), 0)
    owner = (slot_row // 16 == iota((slots, n), 1)).astype(BF16)
    found = dot(owner, order)
    slot_at = iota((slots, packed), 0)
    chosen = found == (slot_at % 8 + 1).astype(F32)
    on_left = slot_at % 16 < 8
    pick_left = jnp.where(chosen & on_left, 1.0, 0.0).astype(BF16)
    pick_right = jnp.where(chosen & ~on_left, 1.0, 0.0).astype(BF16)
    step = 256
    for c in range(half // step):
        left = normed[:, c * step : (c + 1) * step]
        right = normed[:, half + c * step : half + (c + 1) * step]
        out_buf[:, c * step : (c + 1) * step] = (dot(pick_left, left) + dot(pick_right, right)).astype(BF16)

    def block(i):
        return pl.ds(pl.multiple_of(i * 16, 16), 16)

    def exchange(source, target, number, cols):
        group = n // 2
        mine, low = me // group, lax.rem(me, group)

        def send(other):
            pltpu.make_async_remote_copy(
                src_ref=source.at[block(other), cols],
                dst_ref=target.at[block(me), cols],
                send_sem=send_sem.at[number],
                recv_sem=recv_sem.at[number],
                device_id={"ep": other},
                device_id_type=MESH,
            ).start()

        def send_two(i, carry):
            at = lax.rem(low + i, group)
            send((1 - mine) * group + at)
            send(mine * group + at)
            return carry

        send((1 - mine) * group + low)
        lax.fori_loop(1, group, send_two, 0)
        own = pltpu.make_async_copy(
            source.at[block(me), cols], target.at[block(me), cols], local_sem.at[number]
        )
        own.start()
        rest = pl.ds(0, (n - 1) * 16)
        others = pltpu.make_async_remote_copy(
            src_ref=source.at[rest, cols],
            dst_ref=target.at[rest, cols],
            send_sem=send_sem.at[number],
            recv_sem=recv_sem.at[number],
            device_id={"ep": lax.rem(me + 1, n)},
            device_id_type=MESH,
        )
        return own, others

    pl.semaphore_wait(barrier, n - 1)
    first_own, first = exchange(out_buf, in_buf, 0, pl.ds(0, half))
    owner_t = (iota((n, slots), 1) // 16 == iota((n, slots), 0)).astype(BF16)
    lane_slot = iota((packed, slots), 1)
    over = (((0,), (0,)), ((), ()))
    taken = lax.dot_general(order, owner_t, over, preferred_element_type=F32) == (lane_slot % 8 + 1).astype(F32)
    high, low = split(weights)
    lane_left = lane_slot % 16 < 8
    mixing = []
    for part in (high, low):
        value = lax.dot_general(part, owner_t, over, preferred_element_type=F32)
        mixing.append(jnp.where(taken & lane_left, value, 0.0).astype(BF16))
        mixing.append(jnp.where(taken & ~lane_left, value, 0.0).astype(BF16))
    mix = jnp.concatenate(mixing, 0)
    gate_up_copy.wait()
    down_copy.wait()
    first_own.wait()
    first.wait_recv()

    arrived = in_buf[...].astype(F32).reshape(n, 16, half)
    left_in = arrived[:, :8].reshape(n * 8, half).astype(BF16)
    right_in = arrived[:, 8:].reshape(n * 8, half).astype(BF16)
    for c in range(ff // step):
        at = slice(c * step, (c + 1) * step)
        up_at = slice(ff + c * step, ff + (c + 1) * step)
        gate = dot(left_in, gate_up_s[:half, at]) + dot(right_in, gate_up_s[half:, at])
        up = dot(left_in, gate_up_s[:half, up_at]) + dot(right_in, gate_up_s[half:, up_at])
        hidden_s[:, at] = (gate / (1.0 + jnp.exp(-gate)) * up).astype(BF16)
    units = hidden_s[...]
    returns = []
    for c in range(half // step):
        at = slice(c * step, (c + 1) * step)
        right_at = slice(half + c * step, half + (c + 1) * step)
        left = dot(units, down_s[:, at]).reshape(n, 8, step)
        right = dot(units, down_s[:, right_at]).reshape(n, 8, step)
        back_buf[:, at] = jnp.concatenate([left, right], 1).reshape(slots, step).astype(BF16)
        if c % 2:
            returns.append(exchange(back_buf, ret_buf, 1 + c // 2, pl.ds((c - 1) * step, 2 * step)))
    first.wait_send()
    for c in range(half // step):
        if c % 2 == 0:
            returns[c // 2][0].wait()
            returns[c // 2][1].wait_recv()
        at = slice(c * step, (c + 1) * step)
        right_at = slice(half + c * step, half + (c + 1) * step)
        sums = dot(mix, ret_buf[:, at])
        left = sums[:packed] + sums[2 * packed : 3 * packed]
        right = sums[packed : 2 * packed] + sums[3 * packed :]
        for cols, value in ((at, left), (right_at, right)):
            total = (mixed_s[:, cols] + value).astype(BF16)
            out_ref[:, cols] = lax.dot_general(
                place_b, total, over, preferred_element_type=F32
            ).astype(BF16)
    for _, others in returns:
        others.wait_send()


def per_device(
    hidden_in,
    queries,
    key_rows,
    value_rows,
    output_gate,
    decay_rate,
    write_rate,
    state_cache,
    head_gain,
    post_gain,
    routes,
    route_weight,
    w_gate_up,
    w_down,
):
    rows, width = hidden_in.shape
    n = lax.axis_size("ep")
    seqs, heads, head_dim, _ = state_cache.shape
    steps = rows // seqs
    packed = steps * LANE
    ff = w_down.shape[1]
    capacity = max(2, (rows * routes.shape[1] + n - 1) // n)
    assert capacity <= 8 and seqs <= LANE
    vmem = pl.BlockSpec(memory_space=pltpu.VMEM)
    anywhere = pl.BlockSpec(memory_space=pl.ANY)
    wide = pltpu.VMEM((packed, width), F32)
    blocks = pltpu.VMEM((n * 16, width // 2), BF16)
    return pl.pallas_call(
        functools.partial(kernel, n, steps, heads, head_dim),
        out_shape=jax.ShapeDtypeStruct((rows, width), BF16),
        in_specs=[vmem] * 12 + [anywhere] * 2,
        out_specs=vmem,
        scratch_shapes=[wide] * 8
        + [pltpu.VMEM(w_gate_up.shape[1:], BF16), pltpu.VMEM(w_down.shape[1:], BF16)]
        + [blocks] * 4
        + [
            pltpu.VMEM((n * 8, ff), BF16),
            pltpu.SemaphoreType.DMA((2,)),
            pltpu.SemaphoreType.DMA((4,)),
            pltpu.SemaphoreType.DMA((4,)),
            pltpu.SemaphoreType.DMA((4,)),
        ],
        compiler_params=pltpu.CompilerParams(
            collective_id=0, has_side_effects=True, vmem_limit_bytes=56 << 20
        ),
    )(
        hidden_in,
        queries,
        key_rows,
        value_rows,
        output_gate,
        decay_rate.T,
        write_rate.T,
        state_cache,
        head_gain.reshape(1, -1),
        post_gain.reshape(1, -1),
        routes.T,
        route_weight.T,
        w_gate_up,
        w_down,
    )


def solution(mesh):
    split_rows = P(("groups", "ep"), None)
    in_specs = (
        (split_rows,) * 7
        + (P(("groups", "ep"), None, None, None), P(), P(), split_rows, split_rows)
        + (P("ep", None, None), P("ep", None, None))
    )
    return jax.shard_map(
        per_device, mesh=mesh, in_specs=in_specs, out_specs=split_rows, check_vma=False
    )
```

```python
import functools

import jax
import jax.numpy as jnp
from jax import lax
from jax.experimental import pallas as pl
from jax.experimental.pallas import tpu as pltpu
from jax.sharding import PartitionSpec as P

F32 = jnp.float32
BF16 = jnp.bfloat16
LANE = 8
MESH = pl.DeviceIdType.MESH


def iota(shape, dim):
    return lax.broadcasted_iota(jnp.int32, shape, dim)


def exact_dot(a, b, dims=None):
    dims = dims or (((1,), (0,)), ((), ()))
    return lax.dot_general(a, b, dims, precision=lax.Precision.HIGHEST, preferred_element_type=F32)


def dot(a, b):
    return jnp.dot(a, b, preferred_element_type=F32)


def split(value):
    high = value.astype(BF16)
    return high, (value - high.astype(F32)).astype(BF16)


def kernel(
    n,
    steps,
    heads,
    head_dim,
    hidden_ref,
    q_ref,
    k_ref,
    v_ref,
    gate_ref,
    decay_ref,
    write_ref,
    state_hbm,
    head_gain_ref,
    post_gain_ref,
    routes_ref,
    weight_ref,
    gate_up_hbm,
    down_hbm,
    out_ref,
    hid_s,
    q_s,
    k_s,
    v_s,
    gate_s,
    a_s,
    b_s,
    mixed_s,
    gate_up_s,
    down_s,
    state_s,
    product_s,
    out_buf,
    in_buf,
    back_buf,
    ret_buf,
    hidden_s,
    weight_sem,
    local_sem,
    send_sem,
    recv_sem,
):
    me = lax.axis_index("ep")
    rows, width = hidden_ref.shape
    top = routes_ref.shape[0]
    seqs = rows // steps
    packed = steps * LANE
    half = width // 2
    ff = down_s.shape[0]
    state_copy = pltpu.make_async_copy(state_hbm, state_s, weight_sem.at[2])
    state_copy.start()
    barrier = pltpu.get_barrier_semaphore()

    def greet(i, carry):
        pl.semaphore_signal(
            barrier, inc=1, device_id={"ep": lax.rem(me + i, n)}, device_id_type=MESH
        )
        return carry

    lax.fori_loop(1, n, greet, 0)
    gate_up_copy = pltpu.make_async_copy(gate_up_hbm.at[0], gate_up_s, weight_sem.at[0])
    down_copy = pltpu.make_async_copy(down_hbm.at[0], down_s, weight_sem.at[1])
    gate_up_copy.start()
    down_copy.start()

    new_row, old_row = iota((packed, rows), 0), iota((packed, rows), 1)
    place = (old_row // steps == new_row % LANE) & (old_row % steps == new_row // LANE)
    place_f = place.astype(F32)
    place_b = place_f.astype(BF16)
    hid_s[...] = dot(place_b, hidden_ref[...])
    q_s[...] = dot(place_b, q_ref[...])
    k_s[...] = dot(place_b, k_ref[...])
    v_s[...] = dot(place_b, v_ref[...])
    gate_s[...] = dot(place_b, gate_ref[...])
    spread = (iota((heads, width), 1) // head_dim == iota((heads, width), 0)).astype(F32)
    last = (((1,), (1,)), ((), ()))
    a_s[...] = exact_dot(exact_dot(place_f, decay_ref[...], last), spread)
    b_s[...] = exact_dot(exact_dot(place_f, write_ref[...], last), spread)
    gain = head_gain_ref[...]
    sequence = iota((2 * packed, head_dim), 0) % LANE

    def lanes_sum(value):
        return jnp.sum(value, -1, keepdims=True)

    def one_head(h):
        cols = pl.ds(pl.multiple_of(h * head_dim, head_dim), head_dim)
        k_all, q_all = k_s[:, cols], q_s[:, cols]
        both = jnp.concatenate([k_all, q_all], 0).astype(BF16)
        reads = jnp.zeros((2 * packed, head_dim), F32)
        for s in range(seqs):
            reads = jnp.where(sequence == s, dot(both, state_s[s, h]), reads)
        carried = None
        writes, keys = [], []
        for t in range(steps):
            at = slice(t * LANE, (t + 1) * LANE)
            k, q = k_all[at], q_all[at]
            here = pl.ds(t * LANE, LANE)
            a, b, v = a_s[here, cols], b_s[here, cols], v_s[here, cols]
            k_scale = lax.rsqrt(lanes_sum(k * k) + 1e-06)
            q_scale = lax.rsqrt(lanes_sum(q * q) + 1e-06)
            k_read = reads[at] if t == 0 else carried * reads[at]
            for key, w in zip(keys, writes):
                k_read = k_read + lanes_sum(k * key) * w
            new = b * (v - a * (k_scale * k_read))
            carried = a if t == 0 else carried * a
            writes = [w * a for w in writes] + [new * k_scale]
            keys = keys + [k]
            attn = carried * reads[packed + t * LANE : packed + (t + 1) * LANE]
            for key, w in zip(keys, writes):
                attn = attn + lanes_sum(q * key) * w
            attn = attn * q_scale
            norm = lax.rsqrt(lanes_sum(attn * attn) * (1.0 / head_dim) + 1e-06)
            g = gate_s[here, cols]
            mixed_s[here, cols] = hid_s[here, cols] + attn * norm * gain * (g / (1.0 + jnp.exp(-g)))

    def head_group(i, carry):
        for j in range(4):
            one_head(4 * i + j)
        return carry

    state_copy.wait()
    lax.fori_loop(0, heads // 4, head_group, 0)
    mixed = mixed_s[...]
    factor = lax.rsqrt(jnp.sum(mixed * mixed, -1, keepdims=True) * (1.0 / width) + 1e-06)
    normed = (mixed * factor * post_gain_ref[...]).astype(BF16)

    expert = iota((n, rows), 0)
    named = jnp.zeros((n, rows), F32)
    weights = jnp.zeros((n, rows), F32)
    for j in range(top):
        hit = routes_ref[j : j + 1, :] == expert
        named = jnp.where(hit, 1.0, named)
        weights = jnp.where(hit, weight_ref[j : j + 1, :], weights)
    earlier = (iota((rows, rows), 0) <= iota((rows, rows), 1)).astype(BF16)
    order = named * dot(named.astype(BF16), earlier)
    order = lax.dot_general(order.astype(BF16), place_b, last, preferred_element_type=F32).astype(BF16)
    weights = exact_dot(weights, place_f, last)

    slots = n * 16
    slot_row = iota((slots, n), 0)
    owner = (slot_row // 16 == iota((slots, n), 1)).astype(BF16)
    found = dot(owner, order)
    slot_at = iota((slots, packed), 0)
    chosen = found == (slot_at % 8 + 1).astype(F32)
    on_left = slot_at % 16 < 8
    pick_left = jnp.where(chosen & on_left, 1.0, 0.0).astype(BF16)
    pick_right = jnp.where(chosen & ~on_left, 1.0, 0.0).astype(BF16)
    def block(i):
        return pl.ds(pl.multiple_of(i * 16, 16), 16)

    def exchange(source, target, number, cols):
        group = n // 2
        mine, low = me // group, lax.rem(me, group)

        def send(other):
            pltpu.make_async_remote_copy(
                src_ref=source.at[block(other), cols],
                dst_ref=target.at[block(me), cols],
                send_sem=send_sem.at[number],
                recv_sem=recv_sem.at[number],
                device_id={"ep": other},
                device_id_type=MESH,
            ).start()

        def send_two(i, carry):
            at = lax.rem(low + i, group)
            send((1 - mine) * group + at)
            send(mine * group + at)
            return carry

        send((1 - mine) * group + low)
        lax.fori_loop(1, group, send_two, 0)
        own = pltpu.make_async_copy(
            source.at[block(me), cols], target.at[block(me), cols], local_sem.at[number]
        )
        own.start()
        rest = pl.ds(0, (n - 1) * 16)
        others = pltpu.make_async_remote_copy(
            src_ref=source.at[rest, cols],
            dst_ref=target.at[rest, cols],
            send_sem=send_sem.at[number],
            recv_sem=recv_sem.at[number],
            device_id={"ep": lax.rem(me + 1, n)},
            device_id_type=MESH,
        )
        return own, others

    step = half // 4
    parts = ((0, step), (step, 2 * step), (3 * step, step))
    pl.semaphore_wait(barrier, n - 1)
    sent = []
    for number, (start, size) in enumerate(parts):
        left = normed[:, start : start + size]
        right = normed[:, half + start : half + start + size]
        out_buf[:, start : start + size] = (dot(pick_left, left) + dot(pick_right, right)).astype(BF16)
        sent.append(exchange(out_buf, in_buf, number, pl.ds(start, size)))
    owner_t = (iota((n, slots), 1) // 16 == iota((n, slots), 0)).astype(BF16)
    lane_slot = iota((packed, slots), 1)
    over = (((0,), (0,)), ((), ()))
    taken = lax.dot_general(order, owner_t, over, preferred_element_type=F32) == (lane_slot % 8 + 1).astype(F32)
    high, low = split(weights)
    lane_left = lane_slot % 16 < 8
    mixing = []
    for part in (high, low):
        value = lax.dot_general(part, owner_t, over, preferred_element_type=F32)
        mixing.append(jnp.where(taken & lane_left, value, 0.0).astype(BF16))
        mixing.append(jnp.where(taken & ~lane_left, value, 0.0).astype(BF16))
    mix = jnp.concatenate(mixing, 0)
    gate_up_copy.wait()
    down_copy.wait()
    for number, (start, size) in enumerate(parts):
        sent[number][0].wait()
        sent[number][1].wait_recv()
        arrived = in_buf[:, start : start + size].astype(F32).reshape(n, 16, size)
        left_in = arrived[:, :8].reshape(n * 8, size).astype(BF16)
        right_in = arrived[:, 8:].reshape(n * 8, size).astype(BF16)
        left_at, right_at = pl.ds(start, size), pl.ds(half + start, size)

        def product(at):
            value = dot(left_in, gate_up_s[left_at, at]) + dot(right_in, gate_up_s[right_at, at])
            return value if number == 0 else product_s[:, at] + value

        for c in range(ff // step):
            at, up_at = pl.ds(c * step, step), pl.ds(ff + c * step, step)
            gate, up = product(at), product(up_at)
            if number + 1 < len(parts):
                product_s[:, at], product_s[:, up_at] = gate, up
            else:
                hidden_s[:, at] = (gate / (1.0 + jnp.exp(-gate)) * up).astype(BF16)
    units = hidden_s[...]
    returns = []
    for number, (start, size) in enumerate(parts):
        at = slice(start, start + size)
        right_at = slice(half + start, half + start + size)
        left = dot(units, down_s[:, at]).reshape(n, 8, size)
        right = dot(units, down_s[:, right_at]).reshape(n, 8, size)
        back_buf[:, at] = jnp.concatenate([left, right], 1).reshape(slots, size).astype(BF16)
        returns.append(exchange(back_buf, ret_buf, len(parts) + number, pl.ds(start, size)))
    for _, others in sent:
        others.wait_send()
    for number, (start, size) in enumerate(parts):
        returns[number][0].wait()
        returns[number][1].wait_recv()
        at = slice(start, start + size)
        right_at = slice(half + start, half + start + size)
        sums = dot(mix, ret_buf[:, at])
        left = sums[:packed] + sums[2 * packed : 3 * packed]
        right = sums[packed : 2 * packed] + sums[3 * packed :]
        for cols, value in ((at, left), (right_at, right)):
            total = (mixed_s[:, cols] + value).astype(BF16)
            out_ref[:, cols] = lax.dot_general(
                place_b, total, over, preferred_element_type=F32
            ).astype(BF16)
    for _, others in returns:
        others.wait_send()


def per_device(
    hidden_in,
    queries,
    key_rows,
    value_rows,
    output_gate,
    decay_rate,
    write_rate,
    state_cache,
    head_gain,
    post_gain,
    routes,
    route_weight,
    w_gate_up,
    w_down,
):
    rows, width = hidden_in.shape
    n = lax.axis_size("ep")
    seqs, heads, head_dim, _ = state_cache.shape
    steps = rows // seqs
    packed = steps * LANE
    ff = w_down.shape[1]
    capacity = max(2, (rows * routes.shape[1] + n - 1) // n)
    assert capacity <= 8 and seqs <= LANE
    vmem = pl.BlockSpec(memory_space=pltpu.VMEM)
    anywhere = pl.BlockSpec(memory_space=pl.ANY)
    wide = pltpu.VMEM((packed, width), F32)
    blocks = pltpu.VMEM((n * 16, width // 2), BF16)
    return pl.pallas_call(
        functools.partial(kernel, n, steps, heads, head_dim),
        out_shape=jax.ShapeDtypeStruct((rows, width), BF16),
        in_specs=[vmem] * 7 + [anywhere] + [vmem] * 4 + [anywhere] * 2,
        out_specs=vmem,
        scratch_shapes=[wide] * 8
        + [pltpu.VMEM(w_gate_up.shape[1:], BF16), pltpu.VMEM(w_down.shape[1:], BF16)]
        + [pltpu.VMEM(state_cache.shape, BF16), pltpu.VMEM((n * 8, 2 * ff), F32)]
        + [blocks] * 4
        + [
            pltpu.VMEM((n * 8, ff), BF16),
            pltpu.SemaphoreType.DMA((3,)),
            pltpu.SemaphoreType.DMA((6,)),
            pltpu.SemaphoreType.DMA((6,)),
            pltpu.SemaphoreType.DMA((6,)),
        ],
        compiler_params=pltpu.CompilerParams(
            collective_id=0, has_side_effects=True, vmem_limit_bytes=56 << 20
        ),
    )(
        hidden_in,
        queries,
        key_rows,
        value_rows,
        output_gate,
        decay_rate.T,
        write_rate.T,
        state_cache,
        head_gain.reshape(1, -1),
        post_gain.reshape(1, -1),
        routes.T,
        route_weight.T,
        w_gate_up,
        w_down,
    )


def solution(mesh):
    split_rows = P(("groups", "ep"), None)
    in_specs = (
        (split_rows,) * 7
        + (P(("groups", "ep"), None, None, None), P(), P(), split_rows, split_rows)
        + (P("ep", None, None), P("ep", None, None))
    )
    return jax.shard_map(
        per_device, mesh=mesh, in_specs=in_specs, out_specs=split_rows, check_vma=False
    )
```

```python
import functools

import jax
import jax.numpy as jnp
from jax import lax
from jax.experimental import pallas as pl
from jax.experimental.pallas import tpu as pltpu
from jax.sharding import PartitionSpec as P

F32 = jnp.float32
BF16 = jnp.bfloat16
LANE = 8
MESH = pl.DeviceIdType.MESH


def iota(shape, dim):
    return lax.broadcasted_iota(jnp.int32, shape, dim)


def exact_dot(a, b, dims=None):
    dims = dims or (((1,), (0,)), ((), ()))
    return lax.dot_general(a, b, dims, precision=lax.Precision.HIGHEST, preferred_element_type=F32)


def dot(a, b):
    return jnp.dot(a, b, preferred_element_type=F32)


def split(value):
    high = value.astype(BF16)
    return high, (value - high.astype(F32)).astype(BF16)


def kernel(
    n,
    steps,
    heads,
    head_dim,
    hidden_ref,
    q_ref,
    k_ref,
    v_ref,
    gate_ref,
    decay_ref,
    write_ref,
    state_hbm,
    head_gain_ref,
    post_gain_ref,
    routes_ref,
    weight_ref,
    gate_up_hbm,
    down_hbm,
    out_ref,
    hid_s,
    q_s,
    k_s,
    v_s,
    gate_s,
    a_s,
    b_s,
    mixed_s,
    gate_up_s,
    down_s,
    state_s,
    out_buf,
    in_buf,
    back_buf,
    ret_buf,
    hidden_s,
    weight_sem,
    local_sem,
    send_sem,
    recv_sem,
):
    me = lax.axis_index("ep")
    rows, width = hidden_ref.shape
    top = routes_ref.shape[0]
    seqs = rows // steps
    packed = steps * LANE
    half = width // 2
    ff = down_s.shape[0]
    state_copy = pltpu.make_async_copy(state_hbm, state_s, weight_sem.at[2])
    state_copy.start()
    barrier = pltpu.get_barrier_semaphore()

    def greet(i, carry):
        pl.semaphore_signal(
            barrier, inc=1, device_id={"ep": lax.rem(me + i, n)}, device_id_type=MESH
        )
        return carry

    lax.fori_loop(1, n, greet, 0)
    gate_up_copy = pltpu.make_async_copy(gate_up_hbm.at[0], gate_up_s, weight_sem.at[0])
    down_copy = pltpu.make_async_copy(down_hbm.at[0], down_s, weight_sem.at[1])
    gate_up_copy.start()
    down_copy.start()

    new_row, old_row = iota((packed, rows), 0), iota((packed, rows), 1)
    place = (old_row // steps == new_row % LANE) & (old_row % steps == new_row // LANE)
    place_f = place.astype(F32)
    place_b = place_f.astype(BF16)
    hid_s[...] = dot(place_b, hidden_ref[...])
    q_s[...] = dot(place_b, q_ref[...])
    k_s[...] = dot(place_b, k_ref[...])
    v_s[...] = dot(place_b, v_ref[...])
    gate_s[...] = dot(place_b, gate_ref[...])
    spread = (iota((heads, width), 1) // head_dim == iota((heads, width), 0)).astype(F32)
    last = (((1,), (1,)), ((), ()))
    a_s[...] = exact_dot(exact_dot(place_f, decay_ref[...], last), spread)
    b_s[...] = exact_dot(exact_dot(place_f, write_ref[...], last), spread)
    gain = head_gain_ref[...]
    sequence = iota((2 * packed, head_dim), 0) % LANE

    def lanes_sum(value):
        return jnp.sum(value, -1, keepdims=True)

    def one_head(h):
        cols = pl.ds(pl.multiple_of(h * head_dim, head_dim), head_dim)
        k_all, q_all = k_s[:, cols], q_s[:, cols]
        both = jnp.concatenate([k_all, q_all], 0).astype(BF16)
        reads = jnp.zeros((2 * packed, head_dim), F32)
        for s in range(seqs):
            reads = jnp.where(sequence == s, dot(both, state_s[s, h]), reads)
        carried = None
        writes, keys = [], []
        for t in range(steps):
            at = slice(t * LANE, (t + 1) * LANE)
            k, q = k_all[at], q_all[at]
            here = pl.ds(t * LANE, LANE)
            a, b, v = a_s[here, cols], b_s[here, cols], v_s[here, cols]
            k_scale = lax.rsqrt(lanes_sum(k * k) + 1e-06)
            q_scale = lax.rsqrt(lanes_sum(q * q) + 1e-06)
            k_read = reads[at] if t == 0 else carried * reads[at]
            for key, w in zip(keys, writes):
                k_read = k_read + lanes_sum(k * key) * w
            new = b * (v - a * (k_scale * k_read))
            carried = a if t == 0 else carried * a
            writes = [w * a for w in writes] + [new * k_scale]
            keys = keys + [k]
            attn = carried * reads[packed + t * LANE : packed + (t + 1) * LANE]
            for key, w in zip(keys, writes):
                attn = attn + lanes_sum(q * key) * w
            attn = attn * q_scale
            norm = lax.rsqrt(lanes_sum(attn * attn) * (1.0 / head_dim) + 1e-06)
            g = gate_s[here, cols]
            mixed_s[here, cols] = hid_s[here, cols] + attn * norm * gain * (g / (1.0 + jnp.exp(-g)))

    def head_group(i, carry):
        for j in range(4):
            one_head(4 * i + j)
        return carry

    state_copy.wait()
    lax.fori_loop(0, heads // 4, head_group, 0)
    mixed = mixed_s[...]
    factor = lax.rsqrt(jnp.sum(mixed * mixed, -1, keepdims=True) * (1.0 / width) + 1e-06)
    normed = (mixed * factor * post_gain_ref[...]).astype(BF16)

    expert = iota((n, rows), 0)
    named = jnp.zeros((n, rows), F32)
    weights = jnp.zeros((n, rows), F32)
    for j in range(top):
        hit = routes_ref[j : j + 1, :] == expert
        named = jnp.where(hit, 1.0, named)
        weights = jnp.where(hit, weight_ref[j : j + 1, :], weights)
    earlier = (iota((rows, rows), 0) <= iota((rows, rows), 1)).astype(BF16)
    order = named * dot(named.astype(BF16), earlier)
    order = lax.dot_general(order.astype(BF16), place_b, last, preferred_element_type=F32).astype(BF16)
    weights = exact_dot(weights, place_f, last)

    slots = n * 16
    slot_row = iota((slots, n), 0)
    owner = (slot_row // 16 == iota((slots, n), 1)).astype(BF16)
    found = dot(owner, order)
    slot_at = iota((slots, packed), 0)
    chosen = found == (slot_at % 8 + 1).astype(F32)
    on_left = slot_at % 16 < 8
    pick_left = jnp.where(chosen & on_left, 1.0, 0.0).astype(BF16)
    pick_right = jnp.where(chosen & ~on_left, 1.0, 0.0).astype(BF16)
    step = 256
    for c in range(half // step):
        left = normed[:, c * step : (c + 1) * step]
        right = normed[:, half + c * step : half + (c + 1) * step]
        out_buf[:, c * step : (c + 1) * step] = (dot(pick_left, left) + dot(pick_right, right)).astype(BF16)

    def block(i):
        return pl.ds(pl.multiple_of(i * 16, 16), 16)

    def exchange(source, target, number, cols):
        group = n // 2
        mine, low = me // group, lax.rem(me, group)

        def send(other):
            pltpu.make_async_remote_copy(
                src_ref=source.at[block(other), cols],
                dst_ref=target.at[block(me), cols],
                send_sem=send_sem.at[number],
                recv_sem=recv_sem.at[number],
                device_id={"ep": other},
                device_id_type=MESH,
            ).start()

        def send_two(i, carry):
            at = lax.rem(low + i, group)
            send((1 - mine) * group + at)
            send(mine * group + at)
            return carry

        send((1 - mine) * group + low)
        lax.fori_loop(1, group, send_two, 0)
        own = pltpu.make_async_copy(
            source.at[block(me), cols], target.at[block(me), cols], local_sem.at[number]
        )
        own.start()
        rest = pl.ds(0, (n - 1) * 16)
        others = pltpu.make_async_remote_copy(
            src_ref=source.at[rest, cols],
            dst_ref=target.at[rest, cols],
            send_sem=send_sem.at[number],
            recv_sem=recv_sem.at[number],
            device_id={"ep": lax.rem(me + 1, n)},
            device_id_type=MESH,
        )
        return own, others

    pl.semaphore_wait(barrier, n - 1)
    first_own, first = exchange(out_buf, in_buf, 0, pl.ds(0, half))
    owner_t = (iota((n, slots), 1) // 16 == iota((n, slots), 0)).astype(BF16)
    lane_slot = iota((packed, slots), 1)
    over = (((0,), (0,)), ((), ()))
    taken = lax.dot_general(order, owner_t, over, preferred_element_type=F32) == (lane_slot % 8 + 1).astype(F32)
    high, low = split(weights)
    lane_left = lane_slot % 16 < 8
    mixing = []
    for part in (high, low):
        value = lax.dot_general(part, owner_t, over, preferred_element_type=F32)
        mixing.append(jnp.where(taken & lane_left, value, 0.0).astype(BF16))
        mixing.append(jnp.where(taken & ~lane_left, value, 0.0).astype(BF16))
    mix = jnp.concatenate(mixing, 0)
    gate_up_copy.wait()
    down_copy.wait()
    first_own.wait()
    first.wait_recv()

    arrived = in_buf[...].astype(F32).reshape(n, 16, half)
    left_in = arrived[:, :8].reshape(n * 8, half).astype(BF16)
    right_in = arrived[:, 8:].reshape(n * 8, half).astype(BF16)
    for c in range(ff // step):
        at = slice(c * step, (c + 1) * step)
        up_at = slice(ff + c * step, ff + (c + 1) * step)
        gate = dot(left_in, gate_up_s[:half, at]) + dot(right_in, gate_up_s[half:, at])
        up = dot(left_in, gate_up_s[:half, up_at]) + dot(right_in, gate_up_s[half:, up_at])
        hidden_s[:, at] = (gate / (1.0 + jnp.exp(-gate)) * up).astype(BF16)
    units = hidden_s[...]
    for c in range(half // step):
        at = slice(c * step, (c + 1) * step)
        right_at = slice(half + c * step, half + (c + 1) * step)
        left = dot(units, down_s[:, at]).reshape(n, 8, step)
        right = dot(units, down_s[:, right_at]).reshape(n, 8, step)
        back_buf[:, at] = jnp.concatenate([left, right], 1).reshape(slots, step).astype(BF16)
    second_own, second = exchange(back_buf, ret_buf, 1, pl.ds(0, half))
    first.wait_send()
    second_own.wait()
    second.wait_recv()
    for c in range(half // step):
        at = slice(c * step, (c + 1) * step)
        right_at = slice(half + c * step, half + (c + 1) * step)
        sums = dot(mix, ret_buf[:, at])
        left = sums[:packed] + sums[2 * packed : 3 * packed]
        right = sums[packed : 2 * packed] + sums[3 * packed :]
        for cols, value in ((at, left), (right_at, right)):
            total = (mixed_s[:, cols] + value).astype(BF16)
            out_ref[:, cols] = lax.dot_general(
                place_b, total, over, preferred_element_type=F32
            ).astype(BF16)
    second.wait_send()


def per_device(
    hidden_in,
    queries,
    key_rows,
    value_rows,
    output_gate,
    decay_rate,
    write_rate,
    state_cache,
    head_gain,
    post_gain,
    routes,
    route_weight,
    w_gate_up,
    w_down,
):
    rows, width = hidden_in.shape
    n = lax.axis_size("ep")
    seqs, heads, head_dim, _ = state_cache.shape
    steps = rows // seqs
    packed = steps * LANE
    ff = w_down.shape[1]
    capacity = max(2, (rows * routes.shape[1] + n - 1) // n)
    assert capacity <= 8 and seqs <= LANE
    vmem = pl.BlockSpec(memory_space=pltpu.VMEM)
    anywhere = pl.BlockSpec(memory_space=pl.ANY)
    wide = pltpu.VMEM((packed, width), F32)
    blocks = pltpu.VMEM((n * 16, width // 2), BF16)
    return pl.pallas_call(
        functools.partial(kernel, n, steps, heads, head_dim),
        out_shape=jax.ShapeDtypeStruct((rows, width), BF16),
        in_specs=[vmem] * 7 + [anywhere] + [vmem] * 4 + [anywhere] * 2,
        out_specs=vmem,
        scratch_shapes=[wide] * 8
        + [pltpu.VMEM(w_gate_up.shape[1:], BF16), pltpu.VMEM(w_down.shape[1:], BF16)]
        + [pltpu.VMEM(state_cache.shape, BF16)]
        + [blocks] * 4
        + [
            pltpu.VMEM((n * 8, ff), BF16),
            pltpu.SemaphoreType.DMA((3,)),
            pltpu.SemaphoreType.DMA((2,)),
            pltpu.SemaphoreType.DMA((2,)),
            pltpu.SemaphoreType.DMA((2,)),
        ],
        compiler_params=pltpu.CompilerParams(
            collective_id=0, has_side_effects=True, vmem_limit_bytes=56 << 20
        ),
    )(
        hidden_in,
        queries,
        key_rows,
        value_rows,
        output_gate,
        decay_rate.T,
        write_rate.T,
        state_cache,
        head_gain.reshape(1, -1),
        post_gain.reshape(1, -1),
        routes.T,
        route_weight.T,
        w_gate_up,
        w_down,
    )


def solution(mesh):
    split_rows = P(("groups", "ep"), None)
    in_specs = (
        (split_rows,) * 7
        + (P(("groups", "ep"), None, None, None), P(), P(), split_rows, split_rows)
        + (P("ep", None, None), P("ep", None, None))
    )
    return jax.shard_map(
        per_device, mesh=mesh, in_specs=in_specs, out_specs=split_rows, check_vma=False
    )
```

```python
import functools

import jax
import jax.numpy as jnp
from jax import lax
from jax.experimental import pallas as pl
from jax.experimental.pallas import tpu as pltpu
from jax.sharding import PartitionSpec as P

F32 = jnp.float32
BF16 = jnp.bfloat16
LANE = 8
MESH = pl.DeviceIdType.MESH


def iota(shape, dim):
    return lax.broadcasted_iota(jnp.int32, shape, dim)


def exact_dot(a, b, dims=None):
    dims = dims or (((1,), (0,)), ((), ()))
    return lax.dot_general(a, b, dims, precision=lax.Precision.HIGHEST, preferred_element_type=F32)


def dot(a, b):
    return jnp.dot(a, b, preferred_element_type=F32)


def split(value):
    high = value.astype(BF16)
    return high, (value - high.astype(F32)).astype(BF16)


def kernel(
    n,
    steps,
    heads,
    head_dim,
    hidden_ref,
    q_ref,
    k_ref,
    v_ref,
    gate_ref,
    decay_ref,
    write_ref,
    state_hbm,
    head_gain_ref,
    post_gain_ref,
    routes_ref,
    weight_ref,
    gate_up_hbm,
    down_hbm,
    out_ref,
    hid_s,
    q_s,
    k_s,
    v_s,
    gate_s,
    a_s,
    b_s,
    mixed_s,
    gate_up_s,
    down_s,
    state_s,
    out_buf,
    in_buf,
    back_buf,
    ret_buf,
    hidden_s,
    weight_sem,
    local_sem,
    send_sem,
    recv_sem,
):
    me = lax.axis_index("ep")
    rows, width = hidden_ref.shape
    top = routes_ref.shape[0]
    seqs = rows // steps
    packed = steps * LANE
    half = width // 2
    ff = down_s.shape[0]
    state_copy = pltpu.make_async_copy(state_hbm, state_s, weight_sem.at[2])
    state_copy.start()
    barrier = pltpu.get_barrier_semaphore()

    def greet(i, carry):
        pl.semaphore_signal(
            barrier, inc=1, device_id={"ep": lax.rem(me + i, n)}, device_id_type=MESH
        )
        return carry

    lax.fori_loop(1, n, greet, 0)
    gate_up_copy = pltpu.make_async_copy(gate_up_hbm.at[0], gate_up_s, weight_sem.at[0])
    down_copy = pltpu.make_async_copy(down_hbm.at[0], down_s, weight_sem.at[1])
    gate_up_copy.start()
    down_copy.start()

    new_row, old_row = iota((packed, rows), 0), iota((packed, rows), 1)
    place = (old_row // steps == new_row % LANE) & (old_row % steps == new_row // LANE)
    place_f = place.astype(F32)
    place_b = place_f.astype(BF16)
    hid_s[...] = dot(place_b, hidden_ref[...])
    q_s[...] = dot(place_b, q_ref[...])
    k_s[...] = dot(place_b, k_ref[...])
    v_s[...] = dot(place_b, v_ref[...])
    gate_s[...] = dot(place_b, gate_ref[...])
    spread = (iota((heads, width), 1) // head_dim == iota((heads, width), 0)).astype(F32)
    last = (((1,), (1,)), ((), ()))
    a_s[...] = exact_dot(exact_dot(place_f, decay_ref[...], last), spread)
    b_s[...] = exact_dot(exact_dot(place_f, write_ref[...], last), spread)
    gain = head_gain_ref[...]
    sequence = iota((2 * packed, head_dim), 0) % LANE

    def lanes_sum(value):
        return jnp.sum(value, -1, keepdims=True)

    def one_head(h):
        cols = pl.ds(pl.multiple_of(h * head_dim, head_dim), head_dim)
        k_all, q_all = k_s[:, cols], q_s[:, cols]
        both = jnp.concatenate([k_all, q_all], 0).astype(BF16)
        reads = jnp.zeros((2 * packed, head_dim), F32)
        for s in range(seqs):
            reads = jnp.where(sequence == s, dot(both, state_s[s, h]), reads)
        carried = None
        writes, keys = [], []
        for t in range(steps):
            at = slice(t * LANE, (t + 1) * LANE)
            k, q = k_all[at], q_all[at]
            here = pl.ds(t * LANE, LANE)
            a, b, v = a_s[here, cols], b_s[here, cols], v_s[here, cols]
            k_scale = lax.rsqrt(lanes_sum(k * k) + 1e-06)
            q_scale = lax.rsqrt(lanes_sum(q * q) + 1e-06)
            k_read = reads[at] if t == 0 else carried * reads[at]
            for key, w in zip(keys, writes):
                k_read = k_read + lanes_sum(k * key) * w
            new = b * (v - a * (k_scale * k_read))
            carried = a if t == 0 else carried * a
            writes = [w * a for w in writes] + [new * k_scale]
            keys = keys + [k]
            attn = carried * reads[packed + t * LANE : packed + (t + 1) * LANE]
            for key, w in zip(keys, writes):
                attn = attn + lanes_sum(q * key) * w
            attn = attn * q_scale
            norm = lax.rsqrt(lanes_sum(attn * attn) * (1.0 / head_dim) + 1e-06)
            g = gate_s[here, cols]
            mixed_s[here, cols] = hid_s[here, cols] + attn * norm * gain * (g / (1.0 + jnp.exp(-g)))

    def head_group(i, carry):
        for j in range(8):
            one_head(8 * i + j)
        return carry

    state_copy.wait()
    lax.fori_loop(0, heads // 8, head_group, 0)
    mixed = mixed_s[...]
    factor = lax.rsqrt(jnp.sum(mixed * mixed, -1, keepdims=True) * (1.0 / width) + 1e-06)
    normed = (mixed * factor * post_gain_ref[...]).astype(BF16)

    expert = iota((n, rows), 0)
    named = jnp.zeros((n, rows), F32)
    weights = jnp.zeros((n, rows), F32)
    for j in range(top):
        hit = routes_ref[j : j + 1, :] == expert
        named = jnp.where(hit, 1.0, named)
        weights = jnp.where(hit, weight_ref[j : j + 1, :], weights)
    earlier = (iota((rows, rows), 0) <= iota((rows, rows), 1)).astype(BF16)
    order = named * dot(named.astype(BF16), earlier)
    order = lax.dot_general(order.astype(BF16), place_b, last, preferred_element_type=F32).astype(BF16)
    weights = exact_dot(weights, place_f, last)

    slots = n * 16
    slot_row = iota((slots, n), 0)
    owner = (slot_row // 16 == iota((slots, n), 1)).astype(BF16)
    found = dot(owner, order)
    slot_at = iota((slots, packed), 0)
    chosen = found == (slot_at % 8 + 1).astype(F32)
    on_left = slot_at % 16 < 8
    pick_left = jnp.where(chosen & on_left, 1.0, 0.0).astype(BF16)
    pick_right = jnp.where(chosen & ~on_left, 1.0, 0.0).astype(BF16)
    step = 256
    for c in range(half // step):
        left = normed[:, c * step : (c + 1) * step]
        right = normed[:, half + c * step : half + (c + 1) * step]
        out_buf[:, c * step : (c + 1) * step] = (dot(pick_left, left) + dot(pick_right, right)).astype(BF16)

    def block(i):
        return pl.ds(pl.multiple_of(i * 16, 16), 16)

    def exchange(source, target, number, cols):
        group = n // 2
        mine, low = me // group, lax.rem(me, group)

        def send(other):
            pltpu.make_async_remote_copy(
                src_ref=source.at[block(other), cols],
                dst_ref=target.at[block(me), cols],
                send_sem=send_sem.at[number],
                recv_sem=recv_sem.at[number],
                device_id={"ep": other},
                device_id_type=MESH,
            ).start()

        def send_two(i, carry):
            at = lax.rem(low + i, group)
            send((1 - mine) * group + at)
            send(mine * group + at)
            return carry

        send((1 - mine) * group + low)
        lax.fori_loop(1, group, send_two, 0)
        own = pltpu.make_async_copy(
            source.at[block(me), cols], target.at[block(me), cols], local_sem.at[number]
        )
        own.start()
        rest = pl.ds(0, (n - 1) * 16)
        others = pltpu.make_async_remote_copy(
            src_ref=source.at[rest, cols],
            dst_ref=target.at[rest, cols],
            send_sem=send_sem.at[number],
            recv_sem=recv_sem.at[number],
            device_id={"ep": lax.rem(me + 1, n)},
            device_id_type=MESH,
        )
        return own, others

    pl.semaphore_wait(barrier, n - 1)
    first_own, first = exchange(out_buf, in_buf, 0, pl.ds(0, half))
    owner_t = (iota((n, slots), 1) // 16 == iota((n, slots), 0)).astype(BF16)
    lane_slot = iota((packed, slots), 1)
    over = (((0,), (0,)), ((), ()))
    taken = lax.dot_general(order, owner_t, over, preferred_element_type=F32) == (lane_slot % 8 + 1).astype(F32)
    high, low = split(weights)
    lane_left = lane_slot % 16 < 8
    mixing = []
    for part in (high, low):
        value = lax.dot_general(part, owner_t, over, preferred_element_type=F32)
        mixing.append(jnp.where(taken & lane_left, value, 0.0).astype(BF16))
        mixing.append(jnp.where(taken & ~lane_left, value, 0.0).astype(BF16))
    mix = jnp.concatenate(mixing, 0)
    gate_up_copy.wait()
    down_copy.wait()
    first_own.wait()
    first.wait_recv()

    arrived = in_buf[...].astype(F32).reshape(n, 16, half)
    left_in = arrived[:, :8].reshape(n * 8, half).astype(BF16)
    right_in = arrived[:, 8:].reshape(n * 8, half).astype(BF16)
    for c in range(ff // step):
        at = slice(c * step, (c + 1) * step)
        up_at = slice(ff + c * step, ff + (c + 1) * step)
        gate = dot(left_in, gate_up_s[:half, at]) + dot(right_in, gate_up_s[half:, at])
        up = dot(left_in, gate_up_s[:half, up_at]) + dot(right_in, gate_up_s[half:, up_at])
        hidden_s[:, at] = (gate / (1.0 + jnp.exp(-gate)) * up).astype(BF16)
    units = hidden_s[...]
    for c in range(half // step):
        at = slice(c * step, (c + 1) * step)
        right_at = slice(half + c * step, half + (c + 1) * step)
        left = dot(units, down_s[:, at]).reshape(n, 8, step)
        right = dot(units, down_s[:, right_at]).reshape(n, 8, step)
        back_buf[:, at] = jnp.concatenate([left, right], 1).reshape(slots, step).astype(BF16)
    second_own, second = exchange(back_buf, ret_buf, 1, pl.ds(0, half))
    first.wait_send()
    second_own.wait()
    second.wait_recv()
    for c in range(half // step):
        at = slice(c * step, (c + 1) * step)
        right_at = slice(half + c * step, half + (c + 1) * step)
        sums = dot(mix, ret_buf[:, at])
        left = sums[:packed] + sums[2 * packed : 3 * packed]
        right = sums[packed : 2 * packed] + sums[3 * packed :]
        for cols, value in ((at, left), (right_at, right)):
            total = (mixed_s[:, cols] + value).astype(BF16)
            out_ref[:, cols] = lax.dot_general(
                place_b, total, over, preferred_element_type=F32
            ).astype(BF16)
    second.wait_send()


def per_device(
    hidden_in,
    queries,
    key_rows,
    value_rows,
    output_gate,
    decay_rate,
    write_rate,
    state_cache,
    head_gain,
    post_gain,
    routes,
    route_weight,
    w_gate_up,
    w_down,
):
    rows, width = hidden_in.shape
    n = lax.axis_size("ep")
    seqs, heads, head_dim, _ = state_cache.shape
    steps = rows // seqs
    packed = steps * LANE
    ff = w_down.shape[1]
    capacity = max(2, (rows * routes.shape[1] + n - 1) // n)
    assert capacity <= 8 and seqs <= LANE
    vmem = pl.BlockSpec(memory_space=pltpu.VMEM)
    anywhere = pl.BlockSpec(memory_space=pl.ANY)
    wide = pltpu.VMEM((packed, width), F32)
    blocks = pltpu.VMEM((n * 16, width // 2), BF16)
    return pl.pallas_call(
        functools.partial(kernel, n, steps, heads, head_dim),
        out_shape=jax.ShapeDtypeStruct((rows, width), BF16),
        in_specs=[vmem] * 7 + [anywhere] + [vmem] * 4 + [anywhere] * 2,
        out_specs=vmem,
        scratch_shapes=[wide] * 8
        + [pltpu.VMEM(w_gate_up.shape[1:], BF16), pltpu.VMEM(w_down.shape[1:], BF16)]
        + [pltpu.VMEM(state_cache.shape, BF16)]
        + [blocks] * 4
        + [
            pltpu.VMEM((n * 8, ff), BF16),
            pltpu.SemaphoreType.DMA((3,)),
            pltpu.SemaphoreType.DMA((2,)),
            pltpu.SemaphoreType.DMA((2,)),
            pltpu.SemaphoreType.DMA((2,)),
        ],
        compiler_params=pltpu.CompilerParams(
            collective_id=0, has_side_effects=True, vmem_limit_bytes=56 << 20
        ),
    )(
        hidden_in,
        queries,
        key_rows,
        value_rows,
        output_gate,
        decay_rate.T,
        write_rate.T,
        state_cache,
        head_gain.reshape(1, -1),
        post_gain.reshape(1, -1),
        routes.T,
        route_weight.T,
        w_gate_up,
        w_down,
    )


def solution(mesh):
    split_rows = P(("groups", "ep"), None)
    in_specs = (
        (split_rows,) * 7
        + (P(("groups", "ep"), None, None, None), P(), P(), split_rows, split_rows)
        + (P("ep", None, None), P("ep", None, None))
    )
    return jax.shard_map(
        per_device, mesh=mesh, in_specs=in_specs, out_specs=split_rows, check_vma=False
    )
```
